128 devices in a mesh: dp: 4 (over x), expert: 32 (over y, z, core).
Axes of the slice: x: 4, y: 4, z: 4, core: 2. Of those that a mesh axis runs over, the one named last changes fastest.
Arguments:
- tokens: bfloat16 [8192, 7168], P('expert', 'dp'), may hold values from -6 to 6
- cotangent: bfloat16 [8192, 7168], P('expert', 'dp'), may hold values from -6 to 6
- expert_ids: int32 [8192, 8], P('expert'), may hold values from 0 to 255, all different within a row; in each aligned block of 256 rows (0 to 255, 256 to 511, ...) at most 16 rows name the same one
- gate_coef: bfloat16 [8192, 8], P('expert'), may hold values from 0.049804688 to 0.5
- w_gate: bfloat16 [32, 7168, 1024], P('expert', 'dp'), may hold values from -0.0625 to 0.0625
- w_up: bfloat16 [32, 7168, 1024], P('expert', 'dp'), may hold values from -0.0625 to 0.0625
- w_down: bfloat16 [32, 1024, 7168], P('expert', None, 'dp'), may hold values from -0.1875 to 0.1875
Outputs:
- grad_tokens: bfloat16 [8192, 7168], P('expert', 'dp')
- grad_gate: bfloat16 [32, 7168, 1024], P('expert', 'dp')
- grad_up: bfloat16 [32, 7168, 1024], P('expert', 'dp')
- grad_down: bfloat16 [32, 1024, 7168], P('expert', None, 'dp')
The draws below stay inside these ranges and needn't reach their ends.
Inputs may be any that keep to these rules, and one draw needn't show every extreme that they name: `expert_ids`: each row names 8 different experts; the rows of one index of expert (aligned blocks of 256 rows) name any one expert at most 16 times, a bound that some block reaches.
All inputs are finite; a program needn't handle non-finite values.
Results may differ from the reference program's by a relative error of at most 0.022.
Values may be sent and summed in bfloat16 or wider, within the bound.
A program may use at most 128 MiB of HBM per device.

```python
import math
import jax
import jax.numpy as jnp
import numpy as np
from jax import lax

D = 7168
F = 1024
TOP = 8
TOK_DEV = 256
EXPERTS = 32
ALL = 256
CAP = 16
TOKENS = 8192
N_DP = 4
N_EXPERT = 32


def block_scale(stream_key, dims, shards, low, largest):
    def one(dim, blocks):
        heights = jax.random.uniform(jax.random.fold_in(jax.random.fold_in(stream_key, 6), dim), (blocks,), jnp.float32, low / len(shards), largest / len(shards))
        return jnp.repeat(jnp.exp(heights), dims[dim] // blocks).reshape((-1,) + (1,) * (len(dims) - dim - 1))

    loudness = one(*shards[0])
    for cut in shards[1:]:
        loudness = loudness * one(*cut)
    return loudness


def assign_block(own_key, own, number, rows, count, top, most, lean):
    sequence = jax.random.permutation(own_key, count)
    crowded, usual = portions_of(count, rows * top, most, lean, True), portions_of(count, rows * top, most, lean, False)
    places = jnp.arange(count)

    def named(lengths, turn):
        used = int((lengths > 0).sum())
        fixed = max(1, used // 4)
        shifted = fixed + (places - fixed + turn * (used - fixed)) % max(1, count - fixed)
        return jnp.zeros((count,), jnp.int32).at[sequence[jnp.where(places < fixed, places, shifted)]].set(jnp.asarray(lengths, jnp.int32))

    lengths = jnp.where(number % 4 == 0, named(crowded, number // 4), named(usual, number - number // 4 - 1))
    mixed = jax.random.permutation(jax.random.fold_in(own, 3), count)
    donor, taker = mixed[0:count // 2 * 2:2], mixed[1:count // 2 * 2:2]
    room = jnp.minimum(lengths[donor] - 1, most - lengths[taker]) // 2
    room = jnp.where((donor == sequence[0]) | (taker == sequence[0]) | (lengths[taker] == 0), 0, jnp.maximum(room, 0))
    shifted = jax.random.randint(jax.random.fold_in(own, 4), (count // 2,), 0, 1 << 20) % (room + 1)
    lengths = lengths.at[donor].add(-shifted).at[taker].add(shifted)
    members = jnp.searchsorted(jnp.cumsum(lengths), jnp.arange(rows * top), side="right").astype(jnp.int32)
    table = members.reshape(top, rows).T
    table = table[jax.random.permutation(jax.random.fold_in(own, 1), rows)]
    turn = jax.random.randint(jax.random.fold_in(own, 2), (rows, 1), 0, top)
    return jnp.take_along_axis(table, (jnp.arange(top)[None, :] + turn) % top, axis=1)


def portions_of(amount, total, limit, skew, full):
    loads = [(1 << 20) // math.isqrt(grade ** skew) + 1 for grade in range(1, amount + 1)]
    largest = limit if full else min(limit, max(-(-total // amount), total * loads[0] // sum(loads)))
    least = 1 if total - largest >= amount - 1 else 0
    given, surplus = [largest] + [least] * (amount - 1), total - largest - least * (amount - 1)
    while surplus > 0:
        candidates = [i for i in range(1, amount) if given[i] < largest] or [i for i in range(1, amount) if given[i] < limit]
        whole, remaining = sum([loads[i] for i in candidates]), surplus
        for i in candidates:
            addition = min(limit - given[i], max(1, remaining * loads[i] // whole), surplus)
            given[i] = given[i] + addition
            surplus = surplus - addition
    return np.array(given)


def noise(rng, dims, spread, most, shards=(), held_as=jnp.bfloat16):
    drawn = spread * jax.random.normal(rng, dims, jnp.float32)
    if shards:
        drawn = drawn * block_scale(rng, dims, shards, -0.22, 0.18)
    return jnp.clip(drawn, -most, most).astype(held_as)


def setup_inputs(seed: int = 0) -> dict:
    arg_keys = jax.random.split(jax.random.key(seed), 8)
    tokens = noise(arg_keys[0], (TOKENS, D), 1.0, 6.0, ((0, 32), (1, 4)))
    cotangent = noise(arg_keys[1], (TOKENS, D), 1.0, 6.0, ((0, 32), (1, 4)))
    expert_ids_keys = jax.random.split(jax.random.fold_in(arg_keys[2], 1), TOKENS // TOK_DEV)
    expert_ids_turns = jax.random.permutation(jax.random.fold_in(arg_keys[2], 3), TOKENS // TOK_DEV)
    expert_ids = jax.vmap(lambda own, number: assign_block(jax.random.fold_in(arg_keys[2], 2), own, number, TOK_DEV, ALL, TOP, CAP, 2))(expert_ids_keys, expert_ids_turns).reshape((TOKENS, TOP))
    gate_coef = jnp.clip(jnp.exp(math.log(0.5) - 2.306499 * jax.random.uniform(arg_keys[3], (TOKENS, TOP), jnp.float32) ** block_scale(arg_keys[3], (TOKENS, TOP), ((0, 32),), -0.2, 0.2)), 0.049804688, 0.5).astype(jnp.bfloat16)
    w_gate = noise(arg_keys[4], (EXPERTS, D, F), D ** -0.5, 0.0625, ((0, 32), (1, 4)))
    w_up = noise(arg_keys[5], (EXPERTS, D, F), D ** -0.5, 0.0625, ((0, 32), (1, 4)))
    w_down = noise(arg_keys[6], (EXPERTS, F, D), F ** -0.5, 0.1875, ((0, 32), (2, 4)))
    return {"tokens": tokens, "cotangent": cotangent, "expert_ids": expert_ids, "gate_coef": gate_coef, "w_gate": w_gate, "w_up": w_up, "w_down": w_down}


def rounded(tensor):
    return lax.optimization_barrier(tensor.astype(jnp.bfloat16)).astype(jnp.float32)


def split_forward(left_mat, right_mat):
    width = D // N_DP
    summed = jnp.zeros((left_mat.shape[0], right_mat.shape[1]), jnp.float32)
    for quarter_ix in range(N_DP):
        left_part = left_mat[:, quarter_ix * width:(quarter_ix + 1) * width]
        right_part = right_mat[quarter_ix * width:(quarter_ix + 1) * width]
        summed = summed + rounded(jnp.dot(left_part, right_part, preferred_element_type=jnp.float32))
    return summed


def split_backward(left_mat, right_mat):
    width = D // N_DP
    summed = jnp.zeros((left_mat.shape[0], right_mat.shape[0]), jnp.float32)
    for quarter_ix in range(N_DP):
        left_part = left_mat[:, quarter_ix * width:(quarter_ix + 1) * width]
        right_part = right_mat[:, quarter_ix * width:(quarter_ix + 1) * width]
        product = lax.dot_general(left_part, right_part, (((1,), (1,)), ((), ())), preferred_element_type=jnp.float32)
        summed = summed + rounded(product)
    return summed


def reference(tokens, cotangent, expert_ids, gate_coef, w_gate, w_up, w_down):
    max_rows = N_EXPERT * CAP

    def expert_step(running, expert):
        chosen = expert_ids == expert
        picked = jnp.any(chosen, axis=1)
        weight_row = jnp.sum(jnp.where(chosen, gate_coef.astype(jnp.float32), jnp.float32(0.0)), axis=1)
        row_index = jnp.nonzero(picked, size=max_rows, fill_value=0)[0].astype(jnp.int32)
        active = jnp.arange(max_rows, dtype=jnp.int32) < jnp.sum(picked.astype(jnp.int32))
        row_tokens = jnp.where(active[:, None], tokens[row_index], jnp.zeros((), jnp.bfloat16))
        row_cot = cotangent[row_index]
        row_coef = jnp.where(active, weight_row[row_index], jnp.float32(0.0))
        gate_mat = w_gate[expert]
        up_mat = w_up[expert]
        down_mat = w_down[expert]
        gate_pre = split_forward(row_tokens, gate_mat)
        up_pre = split_forward(row_tokens, up_mat)
        squash = jax.nn.sigmoid(gate_pre)
        silu_out = gate_pre * squash
        hidden = (silu_out * up_pre).astype(jnp.bfloat16)
        scaled = (row_coef[:, None] * row_cot.astype(jnp.float32)).astype(jnp.bfloat16)
        grad_down = lax.dot_general(hidden, scaled, (((0,), (0,)), ((), ())), preferred_element_type=jnp.float32).astype(jnp.bfloat16)
        grad_hidden = split_backward(scaled, down_mat)
        back_gate = (grad_hidden * up_pre * squash * (1.0 + gate_pre * (1.0 - squash))).astype(jnp.bfloat16)
        back_up = (grad_hidden * silu_out).astype(jnp.bfloat16)
        grad_gate = lax.dot_general(row_tokens, back_gate, (((0,), (0,)), ((), ())), preferred_element_type=jnp.float32).astype(jnp.bfloat16)
        grad_up = lax.dot_general(row_tokens, back_up, (((0,), (0,)), ((), ())), preferred_element_type=jnp.float32).astype(jnp.bfloat16)
        contrib = lax.dot_general(back_gate, gate_mat, (((1,), (1,)), ((), ())), preferred_element_type=jnp.float32)
        contrib = contrib + lax.dot_general(back_up, up_mat, (((1,), (1,)), ((), ())), preferred_element_type=jnp.float32)
        contrib = contrib.astype(jnp.bfloat16).astype(jnp.float32)
        running = running.at[row_index].add(jnp.where(active[:, None], contrib, jnp.float32(0.0)))
        return running, (grad_gate, grad_up, grad_down)

    start_acc = jnp.zeros((TOKENS, D), jnp.float32)
    running, (grads_gate, grads_up, grads_down) = lax.scan(expert_step, start_acc, jnp.arange(EXPERTS, dtype=jnp.int32))
    return running.astype(jnp.bfloat16), grads_gate, grads_up, grads_down
```

```python
import functools

import jax
import jax.numpy as jnp
from jax import lax
from jax.experimental import pallas as pl
from jax.experimental.pallas import tpu as pltpu
from jax.sharding import PartitionSpec as P

MESH = pl.DeviceIdType.MESH
BF16 = jnp.bfloat16
F32 = jnp.float32
N = 4
CAP = 16
CH = 128


def slot_expert(s, y, z, c):
    d, dy, dc = s >> 7, (s >> 5) & 3, (s >> 4) & 1
    dz = (d - dy) & 3
    return (((y + dy) & 3) << 3) + (((z + dz) & 3) << 1) + ((c + dc) & 1)


def dot(a, b):
    return jnp.dot(a, b, preferred_element_type=F32)


def dot_nt(a, b):
    return lax.dot_general(a, b, (((1,), (1,)), ((), ())), preferred_element_type=F32)


def body(
    tok, cot, ids, coef, wg_h, wu_h, wd_h,
    gt, x_o, c_o, hid_o, bg_o, bu_o,
    wg, wu, wd, st, wt, sel, xs, xr, xf, gu, hh, gu_r, hh_r, ag, ct, rz, ry,
    w_sem, ys, yr, zs, zr, loc, rss, rsr, ags, agr, rzs, rzr, rloc, rys, ryr, xo_sem, ho_sem,
):
    tokens_n = tok.shape[0]
    ff = wg.shape[1]
    x = lax.axis_index("dp")
    e = lax.axis_index("expert")
    y, z, c = lax.div(e, 8), lax.rem(lax.div(e, 2), 4), lax.rem(e, 2)

    def at(dx, dy, dz, dc):
        ny, nz, nc = lax.rem(y + dy, 4), lax.rem(z + dz, 4), lax.rem(c + dc, 2)
        return (lax.rem(x + dx, 4), ny * 8 + nz * 2 + nc)

    weights = [
        pltpu.make_async_copy(src, dst, w_sem.at[i])
        for i, (src, dst) in enumerate(((wg_h, wg), (wu_h, wu), (wd_h, wd)))
    ]
    for w in weights:
        w.start()
    barrier = pltpu.get_barrier_semaphore()
    peers = (
        [(0, k, 0, 0) for k in range(1, 4)]
        + [(0, 0, dz, dc) for dz in range(4) for dc in range(2) if dz or dc]
        + [(k, 0, 0, 0) for k in range(1, 4)]
    )
    for p in peers:
        pl.semaphore_signal(barrier, inc=1, device_id=at(*p), device_id_type=MESH)

    experts = lax.broadcasted_iota(jnp.int32, (tokens_n, 32), 1)
    hot, share = jnp.zeros((tokens_n, 32), F32), jnp.zeros((tokens_n, 32), F32)
    idv, cov = ids[...], coef[...].astype(F32)
    for k in range(ids.shape[1]):
        m = idv[:, k : k + 1] == experts
        hot = hot + jnp.where(m, 1.0, 0.0)
        share = share + jnp.where(m, cov[:, k : k + 1], 0.0)
    hot, share = hot.astype(BF16), share.astype(BF16)
    r_io = lax.broadcasted_iota(jnp.int32, (tokens_n, tokens_n), 0)
    c_io = lax.broadcasted_iota(jnp.int32, (tokens_n, tokens_n), 1)
    before = dot(jnp.where(c_io < r_io, 1.0, 0.0).astype(BF16), hot).astype(BF16)
    slots = N * CH
    s_r = lax.broadcasted_iota(jnp.int32, (slots, 32), 0)
    e_r = lax.broadcasted_iota(jnp.int32, (slots, 32), 1)
    to_slot = jnp.where(slot_expert(s_r, y, z, c) == e_r, 1.0, 0.0).astype(BF16)
    row_r = (lax.broadcasted_iota(jnp.int32, (slots, tokens_n), 0) & 15).astype(F32)
    here = (dot_nt(to_slot, hot) > 0.5) & (dot_nt(to_slot, before) == row_r)
    st[...] = jnp.where(here, 1.0, 0.0).astype(BF16)
    wt[...] = jnp.where(here, dot_nt(to_slot, share), 0.0).astype(BF16)

    def dispatch(a, d):
        mat, rows = ((st, tok), (wt, cot))[a]
        xs[a, d] = dot(mat[d * CH : (d + 1) * CH, :], rows[...]).astype(BF16)

    y_out, z_out, z_loc, rs_out, ag_out = {}, {}, {}, {}, {}
    rz_out, rz_loc, ry_out, outs = {}, {}, {}, []

    def remote(src, dst, send, recv, dev):
        cp = pltpu.make_async_remote_copy(
            src_ref=src, dst_ref=dst, send_sem=send, recv_sem=recv, device_id=dev, device_id_type=MESH
        )
        cp.start()
        return cp

    def send_y(a, d):
        for dy in (2, 1, 3):
            r = pl.ds(dy * 32, 32)
            y_out[a, d, dy] = remote(
                xs.at[a, d, r], xr.at[a, d, r], ys.at[a, d, dy - 1], yr.at[a, d, dy - 1], at(0, dy, 0, 0)
            )

    def send_z(a, d):
        for dy in (0, 1, 3, 2):
            buf = xs if dy == 0 else xr
            if dy:
                y_out[a, d, dy].wait_recv()
            dz = (d - dy) % 4
            for dc in range(2):
                r = pl.ds(dy * 32 + dc * 16, 16)
                if dz == 0 and dc == 0:
                    cp = pltpu.make_async_copy(buf.at[a, d, r], xf.at[a, d, r], loc.at[a, d])
                    cp.start()
                    z_loc[a, d] = cp
                else:
                    i = dy * 2 + dc
                    z_out[a, d, i] = remote(
                        buf.at[a, d, r], xf.at[a, d, r], zs.at[a, d, i], zr.at[a, d, i], at(0, 0, dz, dc)
                    )

    def arrive(a, d):
        z_loc[a, d].wait()
        for i in range(8):
            if (a, d, i) in z_out:
                z_out[a, d, i].wait_recv()
        o = pltpu.make_async_copy(xf.at[a, d], (x_o, c_o)[a].at[pl.ds(d * CH, CH)], xo_sem.at[a, d])
        o.start()
        outs.append(o)

    def scatter(t, d):
        buf, got = ((gu, gu_r), (hh, hh_r))[t]
        for k in (2, 1, 3):
            q = lax.rem(x + k, 4)
            rs_out[t, d, k] = remote(
                buf.at[d, pl.ds(pl.multiple_of(q * 32, 32), 32)],
                got.at[d, k - 1],
                rss.at[t, d, k - 1],
                rsr.at[t, d, k - 1],
                at(k, 0, 0, 0),
            )

    def gate_up(d):
        arrive(0, d)
        if d == 0:
            weights[0].wait()
            weights[1].wait()
        rows = xf[0, d]
        gu[d, :, 0:ff] = dot(rows, wg[...]).astype(BF16)
        gu[d, :, ff : 2 * ff] = dot(rows, wu[...]).astype(BF16)
        scatter(0, d)

    def back(d):
        arrive(1, d)
        if d == 0:
            weights[2].wait()
        hh[d] = dot_nt(xf[1, d], wd[...]).astype(BF16)
        scatter(1, d)

    def finish(d):
        mine = pl.ds(pl.multiple_of(x * 32, 32), 32)
        for t in range(2):
            for k in range(1, 4):
                rs_out[t, d, k].wait_recv()
        pre, gh = gu[d, mine, :].astype(F32), hh[d, mine, :].astype(F32)
        for k in range(3):
            pre = pre + gu_r[d, k].astype(F32)
            gh = gh + hh_r[d, k].astype(F32)
        g, u = pre[:, 0:ff], pre[:, ff : 2 * ff]
        sq = jax.nn.sigmoid(g)
        silu = g * sq
        ag[d, mine, 0:ff] = (silu * u).astype(BF16)
        ag[d, mine, ff : 2 * ff] = (gh * u * sq * (1.0 + g * (1.0 - sq))).astype(BF16)
        ag[d, mine, 2 * ff : 3 * ff] = (gh * silu).astype(BF16)
        for k in (2, 1, 3):
            ag_out[d, k] = remote(
                ag.at[d, mine], ag.at[d, mine], ags.at[d, k - 1], agr.at[d, k - 1], at(k, 0, 0, 0)
            )

    def contrib(d):
        for k in range(1, 4):
            ag_out[d, k].wait_recv()
        for i, o_ref in enumerate((hid_o, bg_o, bu_o)):
            o = pltpu.make_async_copy(
                ag.at[d, :, pl.ds(i * ff, ff)], o_ref.at[pl.ds(d * CH, CH)], ho_sem.at[i, d]
            )
            o.start()
            outs.append(o)
        total = dot_nt(ag[d, :, ff : 2 * ff], wg[...]) + dot_nt(ag[d, :, 2 * ff : 3 * ff], wu[...])
        ct[d] = total.astype(BF16)
        for dy in (2, 1, 3, 0):
            dz = (d - dy) % 4
            land = ry if dy == 0 else rz
            for dc in range(2):
                r = pl.ds(dy * 32 + dc * 16, 16)
                if dz == 0 and dc == 0:
                    cp = pltpu.make_async_copy(ct.at[d, r], land.at[d, r], rloc.at[d])
                    cp.start()
                    rz_loc[d] = cp
                else:
                    i = dy * 2 + dc
                    rz_out[d, i] = remote(
                        ct.at[d, r], land.at[d, r], rzs.at[d, i], rzr.at[d, i], at(0, 0, (4 - dz) % 4, dc)
                    )

    def return_y(d):
        for dy in (2, 1, 3, 0):
            for dc in range(2):
                i = dy * 2 + dc
                if (d, i) in rz_out:
                    rz_out[d, i].wait_recv()
                else:
                    rz_loc[d].wait()
            if dy:
                r = pl.ds(dy * 32, 32)
                ry_out[d, dy] = remote(
                    rz.at[d, r], ry.at[d, r], rys.at[d, dy - 1], ryr.at[d, dy - 1], at(0, 4 - dy, 0, 0)
                )

    dispatch(0, 0)
    pl.semaphore_wait(barrier, len(peers))
    send_y(0, 0)
    dispatch(1, 0)
    send_y(1, 0)
    dispatch(0, 1)
    send_y(0, 1)
    for d in range(1, N):
        for a in range(2):
            if (a, d) != (0, 1):
                dispatch(a, d)
    send_z(0, 0)
    send_y(1, 1)
    send_z(1, 0)
    gate_up(0)
    send_z(0, 1)
    send_y(0, 2)
    back(0)
    send_z(1, 1)
    send_y(1, 2)
    gate_up(1)
    send_z(0, 2)
    send_y(0, 3)
    finish(0)
    back(1)
    send_z(1, 2)
    send_y(1, 3)
    gate_up(2)
    send_z(0, 3)
    finish(1)
    contrib(0)
    back(2)
    send_z(1, 3)
    gate_up(3)
    return_y(0)
    finish(2)
    contrib(1)
    back(3)
    return_y(1)
    finish(3)
    contrib(2)
    s_l = lax.broadcasted_iota(jnp.int32, (32, slots), 1)
    e_l = lax.broadcasted_iota(jnp.int32, (32, slots), 0)
    from_slot = jnp.where(slot_expert(s_l, y, z, c) == e_l, 1.0, 0.0).astype(BF16)
    row_l = (lax.broadcasted_iota(jnp.int32, (tokens_n, slots), 1) & 15).astype(F32)
    here_l = (dot(hot, from_slot) > 0.5) & (dot(before, from_slot) == row_l)
    sel[...] = jnp.where(here_l, 1.0, 0.0).astype(BF16)
    return_y(2)
    contrib(3)
    return_y(3)
    total = None
    for d in range(N):
        for dy in range(1, 4):
            ry_out[d, dy].wait_recv()
        part = dot(sel[:, d * CH : (d + 1) * CH], ry[d])
        total = part if total is None else total + part
    gt[...] = total.astype(BF16)
    for table in (y_out, z_out, rs_out, ag_out, rz_out, ry_out):
        for cp in table.values():
            cp.wait_send()
    for o in outs:
        o.wait()


def local(tokens, cotangent, expert_ids, gate_coef, w_gate, w_up, w_down):
    t_n, dq = tokens.shape
    ff = w_gate.shape[2]
    slots = N * CH
    vm = pl.BlockSpec(memory_space=pltpu.VMEM)
    anym = pl.BlockSpec(memory_space=pl.ANY)
    dma = pltpu.SemaphoreType.DMA
    sds = jax.ShapeDtypeStruct
    gt, x_o, c_o, hid, bg, bu = pl.pallas_call(
        body,
        name="exchange",
        out_shape=(
            sds((t_n, dq), BF16),
            sds((slots, dq), BF16),
            sds((slots, dq), BF16),
            sds((slots, ff), BF16),
            sds((slots, ff), BF16),
            sds((slots, ff), BF16),
        ),
        in_specs=[vm, vm, vm, vm, anym, anym, anym],
        out_specs=(vm, anym, anym, anym, anym, anym),
        scratch_shapes=[
            pltpu.VMEM((dq, ff), BF16),
            pltpu.VMEM((dq, ff), BF16),
            pltpu.VMEM((ff, dq), BF16),
            pltpu.VMEM((slots, t_n), BF16),
            pltpu.VMEM((slots, t_n), BF16),
            pltpu.VMEM((t_n, slots), BF16),
            pltpu.VMEM((2, N, CH, dq), BF16),
            pltpu.VMEM((2, N, CH, dq), BF16),
            pltpu.VMEM((2, N, CH, dq), BF16),
            pltpu.VMEM((N, CH, 2 * ff), BF16),
            pltpu.VMEM((N, CH, ff), BF16),
            pltpu.VMEM((N, 3, 32, 2 * ff), BF16),
            pltpu.VMEM((N, 3, 32, ff), BF16),
            pltpu.VMEM((N, CH, 3 * ff), BF16),
            pltpu.VMEM((N, CH, dq), BF16),
            pltpu.VMEM((N, CH, dq), BF16),
            pltpu.VMEM((N, CH, dq), BF16),
            dma((3,)),
            dma((2, N, 3)),
            dma((2, N, 3)),
            dma((2, N, 8)),
            dma((2, N, 8)),
            dma((2, N)),
            dma((2, N, 3)),
            dma((2, N, 3)),
            dma((N, 3)),
            dma((N, 3)),
            dma((N, 8)),
            dma((N, 8)),
            dma((N,)),
            dma((N, 3)),
            dma((N, 3)),
            dma((2, N)),
            dma((3, N)),
        ],
        compiler_params=pltpu.CompilerParams(
            collective_id=0, has_side_effects=True, vmem_limit_bytes=58 * 2**20
        ),
    )(tokens, cotangent, expert_ids, gate_coef, w_gate[0], w_up[0], w_down[0])
    tn = (((0,), (0,)), ((), ()))
    grad_down = lax.dot_general(hid, c_o, tn, preferred_element_type=F32).astype(BF16)
    grad_gate = lax.dot_general(x_o, bg, tn, preferred_element_type=F32).astype(BF16)
    grad_up = lax.dot_general(x_o, bu, tn, preferred_element_type=F32).astype(BF16)
    return (gt, grad_gate[None], grad_up[None], grad_down[None])


def solution(mesh):
    in_specs = (
        P("expert", "dp"),
        P("expert", "dp"),
        P("expert", None),
        P("expert", None),
        P("expert", "dp", None),
        P("expert", "dp", None),
        P("expert", None, "dp"),
    )
    out_specs = (
        P("expert", "dp"),
        P("expert", "dp", None),
        P("expert", "dp", None),
        P("expert", None, "dp"),
    )
    return jax.shard_map(local, mesh=mesh, in_specs=in_specs, out_specs=out_specs, check_vma=False)
```

```python
import functools

import jax
import jax.numpy as jnp
from jax import lax
from jax.experimental import pallas as pl
from jax.experimental.pallas import tpu as pltpu
from jax.sharding import PartitionSpec as P

MESH = pl.DeviceIdType.MESH
BF16 = jnp.bfloat16
F32 = jnp.float32
N = 4
CAP = 16
CH = 128


def slot_expert(s, y, z, c):
    d, dc, dy = s >> 7, (s >> 6) & 1, (s >> 4) & 3
    dz = (d - dy) & 3
    return (((y + dy) & 3) << 3) + (((z + dz) & 3) << 1) + ((c + dc) & 1)


def dot(a, b):
    return jnp.dot(a, b, preferred_element_type=F32)


def dot_nt(a, b):
    return lax.dot_general(a, b, (((1,), (1,)), ((), ())), preferred_element_type=F32)


def body(
    tok_h, cot_h, ids, coef, wg_h, wu_h, wd_h,
    gt, x_o, c_o, hid_o, bg_o, bu_o,
    tok, cot, wg, wu, wd, st, wt, sel, acc, cs, xs, xr, xf, gu, hh, gu_f, hh_f, gu_n, hh_n, ag, hid, ct, rz, rc, rq,
    w_sem, t_sem, cos, cor, ys, yr, zs, zr, loc, fs, fr, ns, nr, as1, ar1, as2, ar2, hs1, hr1, hs2, hr2,
    rzs, rzr, rloc, rys, ryr, rcs, rcr, xo_sem, ho_sem,
):
    tokens_n, dq = tok.shape
    ff = wg.shape[1]
    x = lax.axis_index("dp")
    e = lax.axis_index("expert")
    y, z, c = lax.div(e, 8), lax.rem(lax.div(e, 2), 4), lax.rem(e, 2)
    xp, xm, xo = lax.rem(x + 1, 4), lax.rem(x + 3, 4), lax.rem(x + 2, 4)

    def at(dx, dy, dz, dc):
        ny, nz, nc = lax.rem(y + dy, 4), lax.rem(z + dz, 4), lax.rem(c + dc, 2)
        return (lax.rem(x + dx, 4), ny * 8 + nz * 2 + nc)

    barrier = pltpu.get_barrier_semaphore()
    peers = (
        [(0, 0, 0, 1)]
        + [(0, k, 0, 0) for k in range(1, 4)]
        + [(0, 0, k, 0) for k in range(1, 4)]
        + [(1, 0, 0, 0), (3, 0, 0, 0)]
    )
    for p in peers:
        pl.semaphore_signal(barrier, inc=1, device_id=at(*p), device_id_type=MESH)

    inputs = [
        pltpu.make_async_copy(src, dst, t_sem.at[i])
        for i, (src, dst) in enumerate(((tok_h, tok), (cot_h, cot)))
    ]
    for i in inputs:
        i.start()
    weights = [
        pltpu.make_async_copy(src, dst, w_sem.at[i])
        for i, (src, dst) in enumerate(((wg_h, wg), (wu_h, wu), (wd_h, wd)))
    ]
    for w in weights:
        w.start()

    experts = lax.broadcasted_iota(jnp.int32, (32, tokens_n), 0)
    hot, share = jnp.zeros((32, tokens_n), F32), jnp.zeros((32, tokens_n), F32)
    idv, cov = ids[...], coef[...].astype(F32)
    for k in range(ids.shape[0]):
        m = idv[k : k + 1, :] == experts
        hot = hot + jnp.where(m, 1.0, 0.0)
        share = share + jnp.where(m, cov[k : k + 1, :], 0.0)
    hot_b, share = hot.astype(BF16), share.astype(BF16)
    r_io = lax.broadcasted_iota(jnp.int32, (tokens_n, tokens_n), 0)
    c_io = lax.broadcasted_iota(jnp.int32, (tokens_n, tokens_n), 1)
    before = dot(hot_b, jnp.where(r_io < c_io, 1.0, 0.0).astype(BF16))
    before_b = before.astype(BF16)
    slots = N * CH
    s_r = lax.broadcasted_iota(jnp.int32, (slots, 32), 0)
    e_r = lax.broadcasted_iota(jnp.int32, (slots, 32), 1)
    to_slot = jnp.where(slot_expert(s_r, y, z, c) == e_r, 1.0, 0.0).astype(BF16)
    row_r = (lax.broadcasted_iota(jnp.int32, (slots, tokens_n), 0) & 15).astype(F32)
    here = (dot(to_slot, hot_b) > 0.5) & (dot(to_slot, before_b) == row_r)
    st[...] = jnp.where(here, 1.0, 0.0).astype(BF16)
    wt[...] = jnp.where(here, dot(to_slot, share), 0.0).astype(BF16)

    core_out, y_out, z_out, z_loc, far, near = {}, {}, {}, {}, {}, {}
    ag1, ag2, hid1, hid2 = {}, {}, {}, {}
    halves = (pl.ds(0, 1024), pl.ds(1024, dq - 1024))
    rz_out, rz_loc, ry_out, rc_out, outs = {}, {}, {}, {}, []

    def remote(table, key, src, dst, send, recv, dev):
        cp = pltpu.make_async_remote_copy(
            src_ref=src, dst_ref=dst, send_sem=send, recv_sem=recv, device_id=dev, device_id_type=MESH
        )
        cp.start()
        table[key] = cp

    def dispatch(a, d):
        mat, rows = ((st, tok), (wt, cot))[a]
        made = dot(mat[d * CH : (d + 1) * CH, :], rows[...]).astype(BF16).reshape(2, 4, CAP, dq)
        xs[a, d, :, 0] = made[0]
        cs[a, d] = made[1]

    def send_core(a, d):
        remote(core_out, (a, d), cs.at[a, d], xs.at[a, d, :, 1], cos.at[a, d], cor.at[a, d], at(0, 0, 0, 1))

    def send_y(a, d):
        core_out[a, d].wait_recv()
        for dy in (2, 1, 3):
            land = xf if dy == d else xr
            remote(
                y_out, (a, d, dy), xs.at[a, d, dy], land.at[a, d, dy],
                ys.at[a, d, dy - 1], yr.at[a, d, dy - 1], at(0, dy, 0, 0),
            )

    def send_z(a, d):
        for dy in (0, 1, 3, 2):
            if dy == d:
                continue
            if dy:
                y_out[a, d, dy].wait_recv()
            remote(
                z_out, (a, d, dy), (xr if dy else xs).at[a, d, dy], xf.at[a, d, dy],
                zs.at[a, d, dy], zr.at[a, d, dy], at(0, 0, (d - dy) % 4, 0),
            )
        if d == 0:
            z_loc[a] = pltpu.make_async_copy(xs.at[a, 0, 0], xf.at[a, 0, 0], loc.at[a])
            z_loc[a].start()

    def arrive(a, d):
        if d == 0:
            z_loc[a].wait()
        else:
            y_out[a, d, d].wait_recv()
        for dy in range(4):
            if dy != d:
                z_out[a, d, dy].wait_recv()
        o = pltpu.make_async_copy(xf.at[a, d], (x_o, c_o)[a].at[d], xo_sem.at[a, d])
        o.start()
        outs.append(o)

    def scatter(t, d):
        buf, f_r, n_r = ((gu, gu_f, gu_n), (hh, hh_f, hh_n))[t]
        for i, dx in ((0, 1), (1, 3)):
            remote(far, (t, d, i), buf.at[d, xo, i], f_r.at[d, i], fs.at[t, d, i], fr.at[t, d, i], at(dx, 0, 0, 0))
        for i, (dx, q) in enumerate(((1, xp), (3, xm))):
            remote(
                near, (t, d, i), buf.at[d, q, 1 - i], n_r.at[d, i, 1 - i],
                ns.at[t, d, i], nr.at[t, d, i], at(dx, 0, 0, 0),
            )

    def scatter_on(t, d):
        buf, f_r, n_r = ((gu, gu_f, gu_n), (hh, hh_f, hh_n))[t]
        for i, (dx, q) in enumerate(((1, xp), (3, xm))):
            far[t, d, i].wait_recv()
            both = buf[d, q, i].astype(F32) + f_r[d, i].astype(F32)
            buf[d, q, i] = both.astype(BF16)
            remote(
                near, (t, d, 2 + i), buf.at[d, q, i], n_r.at[d, i, i],
                ns.at[t, d, 2 + i], nr.at[t, d, 2 + i], at(dx, 0, 0, 0),
            )

    def gate_up(d):
        arrive(0, d)
        if d == 0:
            weights[0].wait()
            weights[1].wait()
        rows = xf[0, d].reshape(CH, dq)
        gu[d, :, :, :, 0:ff] = dot(rows, wg[...]).astype(BF16).reshape(4, 2, CAP, ff)
        gu[d, :, :, :, ff : 2 * ff] = dot(rows, wu[...]).astype(BF16).reshape(4, 2, CAP, ff)
        scatter(0, d)

    def back(d):
        arrive(1, d)
        if d == 0:
            weights[2].wait()
        hh[d] = dot_nt(xf[1, d].reshape(CH, dq), wd[...]).astype(BF16).reshape(4, 2, CAP, ff)
        scatter(1, d)

    def finish(d):
        for t in range(2):
            for i in range(4):
                near[t, d, i].wait_recv()
        pre, gh = gu[d, x].astype(F32), hh[d, x].astype(F32)
        for i in range(2):
            pre = pre + gu_n[d, i].astype(F32)
            gh = gh + hh_n[d, i].astype(F32)
        g, u = pre[:, :, 0:ff], pre[:, :, ff : 2 * ff]
        sq = jax.nn.sigmoid(g)
        silu = g * sq
        hid[d, x] = (silu * u).astype(BF16)
        ag[d, x, :, :, 0:ff] = (gh * u * sq * (1.0 + g * (1.0 - sq))).astype(BF16)
        ag[d, x, :, :, ff : 2 * ff] = (gh * silu).astype(BF16)
        for i, dx in ((0, 1), (1, 3)):
            remote(ag1, (d, i), ag.at[d, x], ag.at[d, x], as1.at[d, i], ar1.at[d, i], at(dx, 0, 0, 0))

    def gather_on(d):
        for i, (dx, q) in enumerate(((1, xm), (3, xp))):
            ag1[d, i].wait_recv()
            remote(ag2, (d, i), ag.at[d, q, i], ag.at[d, q, i], as2.at[d, i], ar2.at[d, i], at(dx, 0, 0, 0))

    def hidden(d):
        for i, dx in ((0, 1), (1, 3)):
            remote(hid1, (d, i), hid.at[d, x], hid.at[d, x], hs1.at[d, i], hr1.at[d, i], at(dx, 0, 0, 0))

    def hidden_on(d):
        for i, (dx, q) in enumerate(((1, xm), (3, xp))):
            hid1[d, i].wait_recv()
            remote(hid2, (d, i), hid.at[d, q, i], hid.at[d, q, i], hs2.at[d, i], hr2.at[d, i], at(dx, 0, 0, 0))

    def keep(src, dst, sem):
        o = pltpu.make_async_copy(src, dst, sem)
        o.start()
        outs.append(o)

    def contrib(d, h):
        if h == 0:
            for i in range(2):
                ag2[d, i].wait_recv()
            for i, o_ref in enumerate((bg_o, bu_o)):
                keep(ag.at[d, :, :, :, pl.ds(i * ff, ff)], o_ref.at[d], ho_sem.at[i, d])
        w = halves[h]
        back_gate = ag[d, :, :, :, 0:ff].reshape(CH, ff)
        back_up = ag[d, :, :, :, ff : 2 * ff].reshape(CH, ff)
        total = dot_nt(back_gate, wg[w, :]) + dot_nt(back_up, wu[w, :])
        ct[d, :, :, :, w] = total.astype(BF16).reshape(4, 2, CAP, w.size)
        for dy in (2, 1, 3, 0):
            dz = (d - dy) % 4
            if dz:
                remote(
                    rz_out, (d, dy, h), ct.at[d, dy, :, :, w], (rz if dy else rc).at[d, dy, :, :, w],
                    rzs.at[d, dy, h], rzr.at[d, dy, h], at(0, 0, 4 - dz, 0),
                )
            elif dy == 0:
                rz_loc[h] = pltpu.make_async_copy(ct.at[d, 0, :, :, w], rc.at[d, 0, :, :, w], rloc.at[h])
                rz_loc[h].start()
            else:
                back_y(ct, d, dy, h)

    def back_y(src, d, dy, h):
        w = halves[h]
        remote(
            ry_out, (d, dy, h), src.at[d, dy, :, :, w], rc.at[d, dy, :, :, w],
            rys.at[d, dy - 1, h], ryr.at[d, dy - 1, h], at(0, 4 - dy, 0, 0),
        )

    def return_y(d, h):
        for dy in (2, 1, 3):
            if dy != d:
                rz_out[d, dy, h].wait_recv()
                back_y(rz, d, dy, h)

    def return_core(d, h):
        if d == 0:
            rz_loc[h].wait()
        else:
            rz_out[d, 0, h].wait_recv()
        for dy in (1, 3, 2):
            ry_out[d, dy, h].wait_recv()
        w = halves[h]
        remote(
            rc_out, (d, h), rc.at[d, :, 1, :, w], rq.at[d, :, :, w], rcs.at[d, h], rcr.at[d, h], at(0, 0, 0, 1)
        )

    def combine(d):
        for h in range(2):
            rc_out[d, h].wait_recv()
        part = dot(sel[:, d * CH : d * CH + 64], rc[d, :, 0].reshape(64, dq))
        part = part + dot(sel[:, d * CH + 64 : (d + 1) * CH], rq[d].reshape(64, dq))
        if d == 0:
            acc[...] = part
        elif d < N - 1:
            acc[...] += part
        else:
            gt[...] = (acc[...] + part).astype(BF16)

    inputs[0].wait()
    dispatch(0, 0)
    pl.semaphore_wait(barrier, len(peers))
    send_core(0, 0)
    inputs[1].wait()
    dispatch(1, 0)
    send_core(1, 0)
    send_y(0, 0)
    dispatch(0, 1)
    send_core(0, 1)
    send_y(1, 0)
    dispatch(1, 1)
    send_core(1, 1)
    send_y(0, 1)
    send_z(0, 0)
    dispatch(0, 2)
    send_core(0, 2)
    send_y(1, 1)
    dispatch(1, 2)
    send_core(1, 2)
    dispatch(0, 3)
    send_core(0, 3)
    dispatch(1, 3)
    send_core(1, 3)
    sel[...] = st[...].astype(F32).T.astype(BF16)
    send_z(1, 0)
    send_y(0, 2)
    gate_up(0)
    send_z(0, 1)
    send_y(1, 2)
    back(0)
    scatter_on(0, 0)
    send_z(1, 1)
    send_y(0, 3)
    scatter_on(1, 0)
    gate_up(1)
    finish(0)
    send_z(0, 2)
    send_y(1, 3)
    back(1)
    scatter_on(0, 1)
    send_z(1, 2)
    gather_on(0)
    scatter_on(1, 1)
    gate_up(2)
    finish(1)
    send_z(0, 3)
    contrib(0, 0)
    back(2)
    contrib(0, 1)
    scatter_on(0, 2)
    send_z(1, 3)
    gather_on(1)
    hidden(0)
    scatter_on(1, 2)
    gate_up(3)
    return_y(0, 0)
    return_y(0, 1)
    back(3)
    finish(2)
    scatter_on(0, 3)
    contrib(1, 0)
    scatter_on(1, 3)
    contrib(1, 1)
    gather_on(2)
    hidden(1)
    hidden_on(0)
    finish(3)
    return_y(1, 0)
    return_y(1, 1)
    contrib(2, 0)
    gather_on(3)
    contrib(2, 1)
    hidden(2)
    hidden(3)
    return_y(2, 0)
    contrib(3, 0)
    return_y(2, 1)
    contrib(3, 1)
    hidden_on(1)
    return_core(0, 0)
    return_core(0, 1)
    return_core(1, 0)
    return_core(1, 1)
    combine(0)
    return_y(3, 0)
    return_y(3, 1)
    hidden_on(2)
    hidden_on(3)
    return_core(2, 0)
    return_core(2, 1)
    combine(1)
    return_core(3, 0)
    return_core(3, 1)
    combine(2)
    combine(3)
    for d in range(N):
        for i in range(2):
            hid2[d, i].wait_recv()
        keep(hid.at[d], hid_o.at[d], ho_sem.at[2, d])
    for table in (core_out, y_out, z_out, far, near, ag1, ag2, hid1, hid2, rz_out, ry_out, rc_out):
        for cp in table.values():
            cp.wait_send()
    for o in outs:
        o.wait()


def grads_body(x_ref, c_ref, hid, bg, bu, gg, gup, gd, hid_t):
    @pl.when(pl.program_id(0) == 0)
    def _():
        hid_t[...] = hid[...].T

    x_t = x_ref[...].T
    gg[...] = dot(x_t, bg[...]).astype(BF16)
    gup[...] = dot(x_t, bu[...]).astype(BF16)
    gd[...] = dot(hid_t[...], c_ref[...]).astype(BF16)


def grads(x_rows, c_rows, hid, bg, bu):
    slots, dq = x_rows.shape
    ff = hid.shape[1]
    tile = 256
    sds = jax.ShapeDtypeStruct
    whole = pl.BlockSpec((slots, ff), lambda i: (0, 0))
    cols = pl.BlockSpec((slots, tile), lambda i: (0, i))
    rows = pl.BlockSpec((tile, ff), lambda i: (i, 0))
    return pl.pallas_call(
        grads_body,
        name="grads",
        grid=(dq // tile,),
        out_shape=(sds((dq, ff), BF16), sds((dq, ff), BF16), sds((ff, dq), BF16)),
        in_specs=[cols, cols, whole, whole, whole],
        out_specs=(rows, rows, pl.BlockSpec((ff, tile), lambda i: (0, i))),
        scratch_shapes=[pltpu.VMEM((ff, slots), BF16)],
        compiler_params=pltpu.CompilerParams(vmem_limit_bytes=60 * 2**20),
    )(x_rows, c_rows, hid, bg, bu)


def local(tokens, cotangent, expert_ids, gate_coef, w_gate, w_up, w_down):
    t_n, dq = tokens.shape
    ff = w_gate.shape[2]
    slots = N * CH
    vm = pl.BlockSpec(memory_space=pltpu.VMEM)
    anym = pl.BlockSpec(memory_space=pl.ANY)
    dma = pltpu.SemaphoreType.DMA
    sds = jax.ShapeDtypeStruct

    def rows(*shape):
        return pltpu.VMEM(shape, BF16)

    block = (4, 2, CAP)
    gt, x_o, c_o, hid, bg, bu = pl.pallas_call(
        body,
        name="exchange",
        out_shape=(
            sds((t_n, dq), BF16),
            sds((N, *block, dq), BF16),
            sds((N, *block, dq), BF16),
            sds((N, *block, ff), BF16),
            sds((N, *block, ff), BF16),
            sds((N, *block, ff), BF16),
        ),
        in_specs=[anym, anym, vm, vm, anym, anym, anym],
        out_specs=(vm, anym, anym, anym, anym, anym),
        scratch_shapes=[
            rows(t_n, dq),
            rows(t_n, dq),
            rows(dq, ff),
            rows(dq, ff),
            rows(ff, dq),
            rows(slots, t_n),
            rows(slots, t_n),
            rows(t_n, slots),
            pltpu.VMEM((t_n, dq), F32),
            rows(2, N, 4, CAP, dq),
            rows(2, N, *block, dq),
            rows(2, N, *block, dq),
            rows(2, N, *block, dq),
            rows(N, *block, 2 * ff),
            rows(N, *block, ff),
            rows(N, 2, CAP, 2 * ff),
            rows(N, 2, CAP, ff),
            rows(N, 2, 2, CAP, 2 * ff),
            rows(N, 2, 2, CAP, ff),
            rows(N, *block, 2 * ff),
            rows(N, *block, ff),
            rows(N, *block, dq),
            rows(N, *block, dq),
            rows(N, *block, dq),
            rows(N, 4, CAP, dq),
            dma((3,)),
            dma((2,)),
            dma((2, N)),
            dma((2, N)),
            dma((2, N, 3)),
            dma((2, N, 3)),
            dma((2, N, 4)),
            dma((2, N, 4)),
            dma((2,)),
            dma((2, N, 2)),
            dma((2, N, 2)),
            dma((2, N, 4)),
            dma((2, N, 4)),
            dma((N, 2)),
            dma((N, 2)),
            dma((N, 2)),
            dma((N, 2)),
            dma((N, 2)),
            dma((N, 2)),
            dma((N, 2)),
            dma((N, 2)),
            dma((N, 4, 2)),
            dma((N, 4, 2)),
            dma((2,)),
            dma((N, 3, 2)),
            dma((N, 3, 2)),
            dma((N, 2)),
            dma((N, 2)),
            dma((2, N)),
            dma((3, N)),
        ],
        compiler_params=pltpu.CompilerParams(
            collective_id=0, has_side_effects=True, vmem_limit_bytes=58 * 2**20
        ),
    )(tokens, cotangent, expert_ids.T, gate_coef.T, w_gate[0], w_up[0], w_down[0])
    grad_gate, grad_up, grad_down = grads(
        x_o.reshape(slots, dq),
        c_o.reshape(slots, dq),
        hid.reshape(slots, ff),
        bg.reshape(slots, ff),
        bu.reshape(slots, ff),
    )
    return (gt, grad_gate[None], grad_up[None], grad_down[None])


def solution(mesh):
    in_specs = (
        P("expert", "dp"),
        P("expert", "dp"),
        P("expert", None),
        P("expert", None),
        P("expert", "dp", None),
        P("expert", "dp", None),
        P("expert", None, "dp"),
    )
    out_specs = (
        P("expert", "dp"),
        P("expert", "dp", None),
        P("expert", "dp", None),
        P("expert", None, "dp"),
    )
    return jax.shard_map(local, mesh=mesh, in_specs=in_specs, out_specs=out_specs, check_vma=False)
```

```python
import functools

import jax
import jax.numpy as jnp
from jax import lax
from jax.experimental import pallas as pl
from jax.experimental.pallas import tpu as pltpu
from jax.sharding import PartitionSpec as P

MESH = pl.DeviceIdType.MESH
BF16 = jnp.bfloat16
F32 = jnp.float32
N = 4
CAP = 16
CH = 128


def slot_expert(s, y, z, c):
    d, dc, dy = s >> 7, (s >> 6) & 1, (s >> 4) & 3
    dz = (d - dy) & 3
    return (((y + dy) & 3) << 3) + (((z + dz) & 3) << 1) + ((c + dc) & 1)


def dot(a, b):
    return jnp.dot(a, b, preferred_element_type=F32)


def dot_nt(a, b):
    return lax.dot_general(a, b, (((1,), (1,)), ((), ())), preferred_element_type=F32)


def body(
    tok_h, cot_h, ids, coef, wg_h, wu_h, wd_h,
    gt, x_o, c_o, hid_o, bg_o, bu_o,
    tok, cot, wg, wu, wd, st, wt, sel, acc, cs, xs, xr, xf, gu, hh, gu_f, hh_f, gu_n, hh_n, ag, hid, ct, rz, rc, rq,
    w_sem, t_sem, cos, cor, ys, yr, zs, zr, loc, fs, fr, ns, nr, as1, ar1, as2, ar2, hs1, hr1, hs2, hr2,
    rzs, rzr, rloc, rys, ryr, rcs, rcr, xo_sem, ho_sem,
):
    tokens_n, dq = tok.shape
    ff = wg.shape[1]
    x = lax.axis_index("dp")
    e = lax.axis_index("expert")
    y, z, c = lax.div(e, 8), lax.rem(lax.div(e, 2), 4), lax.rem(e, 2)
    xp, xm, xo = lax.rem(x + 1, 4), lax.rem(x + 3, 4), lax.rem(x + 2, 4)

    def at(dx, dy, dz, dc):
        ny, nz, nc = lax.rem(y + dy, 4), lax.rem(z + dz, 4), lax.rem(c + dc, 2)
        return (lax.rem(x + dx, 4), ny * 8 + nz * 2 + nc)

    barrier = pltpu.get_barrier_semaphore()
    peers = (
        [(0, 0, 0, 1)]
        + [(0, k, 0, 0) for k in range(1, 4)]
        + [(0, 0, k, 0) for k in range(1, 4)]
        + [(1, 0, 0, 0), (3, 0, 0, 0)]
    )
    for p in peers:
        pl.semaphore_signal(barrier, inc=1, device_id=at(*p), device_id_type=MESH)

    inputs = [
        pltpu.make_async_copy(src, dst, t_sem.at[i])
        for i, (src, dst) in enumerate(((tok_h, tok), (cot_h, cot)))
    ]
    for i in inputs:
        i.start()
    weights = [
        pltpu.make_async_copy(src, dst, w_sem.at[i])
        for i, (src, dst) in enumerate(((wg_h, wg), (wu_h, wu), (wd_h, wd)))
    ]
    for w in weights:
        w.start()

    experts = lax.broadcasted_iota(jnp.int32, (32, tokens_n), 0)
    hot, share = jnp.zeros((32, tokens_n), F32), jnp.zeros((32, tokens_n), F32)
    idv, cov = ids[...], coef[...].astype(F32)
    for k in range(ids.shape[0]):
        m = idv[k : k + 1, :] == experts
        hot = hot + jnp.where(m, 1.0, 0.0)
        share = share + jnp.where(m, cov[k : k + 1, :], 0.0)
    hot_b, share = hot.astype(BF16), share.astype(BF16)
    r_io = lax.broadcasted_iota(jnp.int32, (tokens_n, tokens_n), 0)
    c_io = lax.broadcasted_iota(jnp.int32, (tokens_n, tokens_n), 1)
    before = dot(hot_b, jnp.where(r_io < c_io, 1.0, 0.0).astype(BF16))
    before_b = before.astype(BF16)
    slots = N * CH
    s_r = lax.broadcasted_iota(jnp.int32, (slots, 32), 0)
    e_r = lax.broadcasted_iota(jnp.int32, (slots, 32), 1)
    to_slot = jnp.where(slot_expert(s_r, y, z, c) == e_r, 1.0, 0.0).astype(BF16)
    row_r = (lax.broadcasted_iota(jnp.int32, (slots, tokens_n), 0) & 15).astype(F32)
    here = (dot(to_slot, hot_b) > 0.5) & (dot(to_slot, before_b) == row_r)
    st[...] = jnp.where(here, 1.0, 0.0).astype(BF16)
    wt[...] = jnp.where(here, dot(to_slot, share), 0.0).astype(BF16)

    core_out, y_out, z_out, z_loc, far, near = {}, {}, {}, {}, {}, {}
    ag1, ag2, hid1, hid2 = {}, {}, {}, {}
    halves = (pl.ds(0, 1024), pl.ds(1024, dq - 1024))
    route = (pl.ds(0, dq // 2), pl.ds(dq // 2, dq // 2))
    rz_out, rz_loc, ry_out, rc_out, outs = {}, {}, {}, {}, []

    def remote(table, key, src, dst, send, recv, dev):
        cp = pltpu.make_async_remote_copy(
            src_ref=src, dst_ref=dst, send_sem=send, recv_sem=recv, device_id=dev, device_id_type=MESH
        )
        cp.start()
        table[key] = cp

    def dispatch(a, d):
        mat, rows = ((st, tok), (wt, cot))[a]
        made = dot(mat[d * CH : (d + 1) * CH, :], rows[...]).astype(BF16).reshape(2, 4, CAP, dq)
        xs[a, d, :, 0] = made[0]
        cs[a, d] = made[1]

    def send_core(a, d):
        remote(core_out, (a, d), cs.at[a, d], xs.at[a, d, :, 1], cos.at[a, d], cor.at[a, d], at(0, 0, 0, 1))

    def hop(axis, k):
        return at(0, k, 0, 0) if axis == 0 else at(0, 0, k, 0)

    def paths(d):
        for dy in (2, 1, 3, 0):
            off = (dy, (d - dy) % 4)
            for r in range(2):
                yield dy, r, off[r], off[1 - r]

    def send_y(a, d):
        core_out[a, d].wait_recv()
        for dy, r, f, g in paths(d):
            if f:
                w = route[r]
                remote(
                    y_out, (a, d, dy, r), xs.at[a, d, dy, :, :, w], (xr if g else xf).at[a, d, dy, :, :, w],
                    ys.at[a, d, dy, r], yr.at[a, d, dy, r], hop(r, f),
                )

    def send_z(a, d):
        if d == 0:
            z_loc[a] = pltpu.make_async_copy(xs.at[a, 0, 0], xf.at[a, 0, 0], loc.at[a])
            z_loc[a].start()
        for dy, r, f, g in sorted(paths(d), key=lambda p: p[2] % 4 == 2):
            if g:
                if f:
                    y_out[a, d, dy, r].wait_recv()
                w = route[r]
                remote(
                    z_out, (a, d, dy, r), (xr if f else xs).at[a, d, dy, :, :, w], xf.at[a, d, dy, :, :, w],
                    zs.at[a, d, dy, r], zr.at[a, d, dy, r], hop(1 - r, g),
                )

    def arrive(a, d):
        if d == 0:
            z_loc[a].wait()
        for dy, r, f, g in paths(d):
            if g:
                z_out[a, d, dy, r].wait_recv()
            elif f:
                y_out[a, d, dy, r].wait_recv()
        o = pltpu.make_async_copy(xf.at[a, d], (x_o, c_o)[a].at[d], xo_sem.at[a, d])
        o.start()
        outs.append(o)

    def scatter(t, d):
        buf, f_r, n_r = ((gu, gu_f, gu_n), (hh, hh_f, hh_n))[t]
        for i, dx in ((0, 1), (1, 3)):
            remote(far, (t, d, i), buf.at[d, xo, i], f_r.at[d, i], fs.at[t, d, i], fr.at[t, d, i], at(dx, 0, 0, 0))
        for i, (dx, q) in enumerate(((1, xp), (3, xm))):
            remote(
                near, (t, d, i), buf.at[d, q, 1 - i], n_r.at[d, i, 1 - i],
                ns.at[t, d, i], nr.at[t, d, i], at(dx, 0, 0, 0),
            )

    def scatter_on(t, d):
        buf, f_r, n_r = ((gu, gu_f, gu_n), (hh, hh_f, hh_n))[t]
        for i, (dx, q) in enumerate(((1, xp), (3, xm))):
            far[t, d, i].wait_recv()
            both = buf[d, q, i].astype(F32) + f_r[d, i].astype(F32)
            buf[d, q, i] = both.astype(BF16)
            remote(
                near, (t, d, 2 + i), buf.at[d, q, i], n_r.at[d, i, i],
                ns.at[t, d, 2 + i], nr.at[t, d, 2 + i], at(dx, 0, 0, 0),
            )

    def gate_up(d):
        arrive(0, d)
        if d == 0:
            weights[0].wait()
            weights[1].wait()
        rows = xf[0, d].reshape(CH, dq)
        gu[d, :, :, :, 0:ff] = dot(rows, wg[...]).astype(BF16).reshape(4, 2, CAP, ff)
        gu[d, :, :, :, ff : 2 * ff] = dot(rows, wu[...]).astype(BF16).reshape(4, 2, CAP, ff)
        scatter(0, d)

    def back(d):
        arrive(1, d)
        if d == 0:
            weights[2].wait()
        hh[d] = dot_nt(xf[1, d].reshape(CH, dq), wd[...]).astype(BF16).reshape(4, 2, CAP, ff)
        scatter(1, d)

    def finish(d):
        for t in range(2):
            for i in range(4):
                near[t, d, i].wait_recv()
        pre, gh = gu[d, x].astype(F32), hh[d, x].astype(F32)
        for i in range(2):
            pre = pre + gu_n[d, i].astype(F32)
            gh = gh + hh_n[d, i].astype(F32)
        g, u = pre[:, :, 0:ff], pre[:, :, ff : 2 * ff]
        sq = jax.nn.sigmoid(g)
        silu = g * sq
        hid[d, x] = (silu * u).astype(BF16)
        ag[d, x, :, :, 0:ff] = (gh * u * sq * (1.0 + g * (1.0 - sq))).astype(BF16)
        ag[d, x, :, :, ff : 2 * ff] = (gh * silu).astype(BF16)
        for i, dx in ((0, 1), (1, 3)):
            remote(ag1, (d, i), ag.at[d, x], ag.at[d, x], as1.at[d, i], ar1.at[d, i], at(dx, 0, 0, 0))

    def gather_on(d):
        for i, (dx, q) in enumerate(((1, xm), (3, xp))):
            ag1[d, i].wait_recv()
            remote(ag2, (d, i), ag.at[d, q, i], ag.at[d, q, i], as2.at[d, i], ar2.at[d, i], at(dx, 0, 0, 0))

    def hidden(d):
        for i, dx in ((0, 1), (1, 3)):
            remote(hid1, (d, i), hid.at[d, x], hid.at[d, x], hs1.at[d, i], hr1.at[d, i], at(dx, 0, 0, 0))

    def hidden_on(d):
        for i, (dx, q) in enumerate(((1, xm), (3, xp))):
            hid1[d, i].wait_recv()
            remote(hid2, (d, i), hid.at[d, q, i], hid.at[d, q, i], hs2.at[d, i], hr2.at[d, i], at(dx, 0, 0, 0))

    def keep(src, dst, sem):
        o = pltpu.make_async_copy(src, dst, sem)
        o.start()
        outs.append(o)

    def contrib(d, h):
        if h == 0:
            for i in range(2):
                ag2[d, i].wait_recv()
            for i, o_ref in enumerate((bg_o, bu_o)):
                keep(ag.at[d, :, :, :, pl.ds(i * ff, ff)], o_ref.at[d], ho_sem.at[i, d])
        w = halves[h]
        back_gate = ag[d, :, :, :, 0:ff].reshape(CH, ff)
        back_up = ag[d, :, :, :, ff : 2 * ff].reshape(CH, ff)
        total = dot_nt(back_gate, wg[w, :]) + dot_nt(back_up, wu[w, :])
        ct[d, :, :, :, w] = total.astype(BF16).reshape(4, 2, CAP, w.size)
        for dy, f, g in ways_back(d, h):
            if f:
                remote(
                    rz_out, (d, dy, h), ct.at[d, dy, :, :, w], (rz if g else rc).at[d, dy, :, :, w],
                    rzs.at[d, dy, h], rzr.at[d, dy, h], hop(1 - h, 4 - f),
                )
            elif g:
                second_back(ct, d, dy, h, g)
            else:
                rz_loc[h] = pltpu.make_async_copy(ct.at[d, 0, :, :, w], rc.at[d, 0, :, :, w], rloc.at[h])
                rz_loc[h].start()

    def ways_back(d, h):
        for dy in (2, 1, 3, 0):
            off = ((d - dy) % 4, dy)
            yield dy, off[h], off[1 - h]

    def second_back(src, d, dy, h, g):
        w = halves[h]
        remote(
            ry_out, (d, dy, h), src.at[d, dy, :, :, w], rc.at[d, dy, :, :, w],
            rys.at[d, dy, h], ryr.at[d, dy, h], hop(h, 4 - g),
        )

    def return_y(d, h):
        for dy, f, g in sorted(ways_back(d, h), key=lambda p: p[1] == 2):
            if f and g:
                rz_out[d, dy, h].wait_recv()
                second_back(rz, d, dy, h, g)

    def return_core(d, h):
        for dy, f, g in ways_back(d, h):
            if g:
                ry_out[d, dy, h].wait_recv()
            elif f:
                rz_out[d, dy, h].wait_recv()
            else:
                rz_loc[h].wait()
        w = halves[h]
        remote(
            rc_out, (d, h), rc.at[d, :, 1, :, w], rq.at[d, :, :, w], rcs.at[d, h], rcr.at[d, h], at(0, 0, 0, 1)
        )

    def combine(d):
        for h in range(2):
            rc_out[d, h].wait_recv()
        part = dot(sel[:, d * CH : d * CH + 64], rc[d, :, 0].reshape(64, dq))
        part = part + dot(sel[:, d * CH + 64 : (d + 1) * CH], rq[d].reshape(64, dq))
        if d == 0:
            acc[...] = part
        elif d < N - 1:
            acc[...] += part
        else:
            gt[...] = (acc[...] + part).astype(BF16)

    inputs[0].wait()
    dispatch(0, 0)
    pl.semaphore_wait(barrier, len(peers))
    send_core(0, 0)
    inputs[1].wait()
    dispatch(1, 0)
    send_core(1, 0)
    send_y(0, 0)
    dispatch(0, 1)
    send_core(0, 1)
    send_y(1, 0)
    dispatch(1, 1)
    send_core(1, 1)
    send_y(0, 1)
    send_z(0, 0)
    dispatch(0, 2)
    send_core(0, 2)
    send_y(1, 1)
    dispatch(1, 2)
    send_core(1, 2)
    dispatch(0, 3)
    send_core(0, 3)
    dispatch(1, 3)
    send_core(1, 3)
    sel[...] = st[...].astype(F32).T.astype(BF16)
    send_z(1, 0)
    send_y(0, 2)
    gate_up(0)
    send_z(0, 1)
    send_y(1, 2)
    back(0)
    scatter_on(0, 0)
    send_z(1, 1)
    send_y(0, 3)
    scatter_on(1, 0)
    gate_up(1)
    finish(0)
    send_z(0, 2)
    send_y(1, 3)
    back(1)
    scatter_on(0, 1)
    send_z(1, 2)
    gather_on(0)
    scatter_on(1, 1)
    gate_up(2)
    finish(1)
    send_z(0, 3)
    contrib(0, 0)
    back(2)
    contrib(0, 1)
    scatter_on(0, 2)
    send_z(1, 3)
    gather_on(1)
    hidden(0)
    scatter_on(1, 2)
    gate_up(3)
    return_y(0, 0)
    return_y(0, 1)
    back(3)
    finish(2)
    scatter_on(0, 3)
    contrib(1, 0)
    scatter_on(1, 3)
    contrib(1, 1)
    gather_on(2)
    hidden(1)
    hidden_on(0)
    finish(3)
    return_y(1, 0)
    return_y(1, 1)
    contrib(2, 0)
    gather_on(3)
    contrib(2, 1)
    hidden(2)
    hidden(3)
    return_y(2, 0)
    contrib(3, 0)
    return_y(2, 1)
    contrib(3, 1)
    hidden_on(1)
    return_core(0, 0)
    return_core(0, 1)
    return_core(1, 0)
    return_core(1, 1)
    combine(0)
    return_y(3, 0)
    return_y(3, 1)
    hidden_on(2)
    hidden_on(3)
    return_core(2, 0)
    return_core(2, 1)
    combine(1)
    return_core(3, 0)
    return_core(3, 1)
    combine(2)
    combine(3)
    for d in range(N):
        for i in range(2):
            hid2[d, i].wait_recv()
        keep(hid.at[d], hid_o.at[d], ho_sem.at[2, d])
    for table in (core_out, y_out, z_out, far, near, ag1, ag2, hid1, hid2, rz_out, ry_out, rc_out):
        for cp in table.values():
            cp.wait_send()
    for o in outs:
        o.wait()


def grads_body(x_ref, c_ref, hid, bg, bu, gg, gup, gd, hid_t):
    @pl.when(pl.program_id(0) == 0)
    def _():
        hid_t[...] = hid[...].T

    x_t = x_ref[...].T
    gg[...] = dot(x_t, bg[...]).astype(BF16)
    gup[...] = dot(x_t, bu[...]).astype(BF16)
    gd[...] = dot(hid_t[...], c_ref[...]).astype(BF16)


def grads(x_rows, c_rows, hid, bg, bu):
    slots, dq = x_rows.shape
    ff = hid.shape[1]
    tile = 256
    sds = jax.ShapeDtypeStruct
    whole = pl.BlockSpec((slots, ff), lambda i: (0, 0))
    cols = pl.BlockSpec((slots, tile), lambda i: (0, i))
    rows = pl.BlockSpec((tile, ff), lambda i: (i, 0))
    return pl.pallas_call(
        grads_body,
        name="grads",
        grid=(dq // tile,),
        out_shape=(sds((dq, ff), BF16), sds((dq, ff), BF16), sds((ff, dq), BF16)),
        in_specs=[cols, cols, whole, whole, whole],
        out_specs=(rows, rows, pl.BlockSpec((ff, tile), lambda i: (0, i))),
        scratch_shapes=[pltpu.VMEM((ff, slots), BF16)],
        compiler_params=pltpu.CompilerParams(vmem_limit_bytes=60 * 2**20),
    )(x_rows, c_rows, hid, bg, bu)


def local(tokens, cotangent, expert_ids, gate_coef, w_gate, w_up, w_down):
    t_n, dq = tokens.shape
    ff = w_gate.shape[2]
    slots = N * CH
    vm = pl.BlockSpec(memory_space=pltpu.VMEM)
    anym = pl.BlockSpec(memory_space=pl.ANY)
    dma = pltpu.SemaphoreType.DMA
    sds = jax.ShapeDtypeStruct

    def rows(*shape):
        return pltpu.VMEM(shape, BF16)

    block = (4, 2, CAP)
    gt, x_o, c_o, hid, bg, bu = pl.pallas_call(
        body,
        name="exchange",
        out_shape=(
            sds((t_n, dq), BF16),
            sds((N, *block, dq), BF16),
            sds((N, *block, dq), BF16),
            sds((N, *block, ff), BF16),
            sds((N, *block, ff), BF16),
            sds((N, *block, ff), BF16),
        ),
        in_specs=[anym, anym, vm, vm, anym, anym, anym],
        out_specs=(vm, anym, anym, anym, anym, anym),
        scratch_shapes=[
            rows(t_n, dq),
            rows(t_n, dq),
            rows(dq, ff),
            rows(dq, ff),
            rows(ff, dq),
            rows(slots, t_n),
            rows(slots, t_n),
            rows(t_n, slots),
            pltpu.VMEM((t_n, dq), F32),
            rows(2, N, 4, CAP, dq),
            rows(2, N, *block, dq),
            rows(2, N, *block, dq),
            rows(2, N, *block, dq),
            rows(N, *block, 2 * ff),
            rows(N, *block, ff),
            rows(N, 2, CAP, 2 * ff),
            rows(N, 2, CAP, ff),
            rows(N, 2, 2, CAP, 2 * ff),
            rows(N, 2, 2, CAP, ff),
            rows(N, *block, 2 * ff),
            rows(N, *block, ff),
            rows(N, *block, dq),
            rows(N, *block, dq),
            rows(N, *block, dq),
            rows(N, 4, CAP, dq),
            dma((3,)),
            dma((2,)),
            dma((2, N)),
            dma((2, N)),
            dma((2, N, 4, 2)),
            dma((2, N, 4, 2)),
            dma((2, N, 4, 2)),
            dma((2, N, 4, 2)),
            dma((2,)),
            dma((2, N, 2)),
            dma((2, N, 2)),
            dma((2, N, 4)),
            dma((2, N, 4)),
            dma((N, 2)),
            dma((N, 2)),
            dma((N, 2)),
            dma((N, 2)),
            dma((N, 2)),
            dma((N, 2)),
            dma((N, 2)),
            dma((N, 2)),
            dma((N, 4, 2)),
            dma((N, 4, 2)),
            dma((2,)),
            dma((N, 4, 2)),
            dma((N, 4, 2)),
            dma((N, 2)),
            dma((N, 2)),
            dma((2, N)),
            dma((3, N)),
        ],
        compiler_params=pltpu.CompilerParams(
            collective_id=0, has_side_effects=True, vmem_limit_bytes=58 * 2**20
        ),
    )(tokens, cotangent, expert_ids.T, gate_coef.T, w_gate[0], w_up[0], w_down[0])
    grad_gate, grad_up, grad_down = grads(
        x_o.reshape(slots, dq),
        c_o.reshape(slots, dq),
        hid.reshape(slots, ff),
        bg.reshape(slots, ff),
        bu.reshape(slots, ff),
    )
    return (gt, grad_gate[None], grad_up[None], grad_down[None])


def solution(mesh):
    in_specs = (
        P("expert", "dp"),
        P("expert", "dp"),
        P("expert", None),
        P("expert", None),
        P("expert", "dp", None),
        P("expert", "dp", None),
        P("expert", None, "dp"),
    )
    out_specs = (
        P("expert", "dp"),
        P("expert", "dp", None),
        P("expert", "dp", None),
        P("expert", None, "dp"),
    )
    return jax.shard_map(local, mesh=mesh, in_specs=in_specs, out_specs=out_specs, check_vma=False)
```

```python
import functools

import jax
import jax.numpy as jnp
from jax import lax
from jax.experimental import pallas as pl
from jax.experimental.pallas import tpu as pltpu
from jax.sharding import PartitionSpec as P

MESH = pl.DeviceIdType.MESH
BF16 = jnp.bfloat16
F32 = jnp.float32
N = 4
CAP = 16
CH = 128


def slot_expert(s, y, z, c):
    d, dc, dy = s >> 7, (s >> 6) & 1, (s >> 4) & 3
    dz = (d - dy) & 3
    return (((y + dy) & 3) << 3) + (((z + dz) & 3) << 1) + ((c + dc) & 1)


def dot(a, b):
    return jnp.dot(a, b, preferred_element_type=F32)


def dot_nt(a, b):
    return lax.dot_general(a, b, (((1,), (1,)), ((), ())), preferred_element_type=F32)


def body(
    tok_h, cot_h, ids, coef, wg_h, wu_h, wd_h,
    gt, x_o, c_o, hid_o, bg_o, bu_o,
    tok, cot, wg, wu, wd, st, wt, sel, acc, cs, xs, xr, xf, gu, hh, gu_f, hh_f, gu_n, hh_n, ag, hid, ct, rz, rc, rq,
    w_sem, t_sem, cos, cor, ys, yr, zs, zr, loc, fs, fr, ns, nr, as1, ar1, as2, ar2, hs1, hr1, hs2, hr2,
    rzs, rzr, rloc, rys, ryr, rcs, rcr, xo_sem, ho_sem,
):
    tokens_n, dq = tok.shape
    ff = wg.shape[1]
    x = lax.axis_index("dp")
    e = lax.axis_index("expert")
    y, z, c = lax.div(e, 8), lax.rem(lax.div(e, 2), 4), lax.rem(e, 2)
    xp, xm, xo = lax.rem(x + 1, 4), lax.rem(x + 3, 4), lax.rem(x + 2, 4)

    def at(dx, dy, dz, dc):
        ny, nz, nc = lax.rem(y + dy, 4), lax.rem(z + dz, 4), lax.rem(c + dc, 2)
        return (lax.rem(x + dx, 4), ny * 8 + nz * 2 + nc)

    barrier = pltpu.get_barrier_semaphore()
    peers = (
        [(0, 0, 0, 1)]
        + [(0, k, 0, 0) for k in range(1, 4)]
        + [(0, 0, k, 0) for k in range(1, 4)]
        + [(1, 0, 0, 0), (3, 0, 0, 0)]
    )
    for p in peers:
        pl.semaphore_signal(barrier, inc=1, device_id=at(*p), device_id_type=MESH)

    inputs = [
        pltpu.make_async_copy(src, dst, t_sem.at[i])
        for i, (src, dst) in enumerate(((tok_h, tok), (cot_h, cot)))
    ]
    for i in inputs:
        i.start()
    weights = [
        pltpu.make_async_copy(src, dst, w_sem.at[i])
        for i, (src, dst) in enumerate(((wg_h, wg), (wu_h, wu), (wd_h, wd)))
    ]
    for w in weights:
        w.start()

    experts = lax.broadcasted_iota(jnp.int32, (32, tokens_n), 0)
    hot, share = jnp.zeros((32, tokens_n), F32), jnp.zeros((32, tokens_n), F32)
    idv, cov = ids[...], coef[...].astype(F32)
    for k in range(ids.shape[0]):
        m = idv[k : k + 1, :] == experts
        hot = hot + jnp.where(m, 1.0, 0.0)
        share = share + jnp.where(m, cov[k : k + 1, :], 0.0)
    hot_b, share = hot.astype(BF16), share.astype(BF16)
    r_io = lax.broadcasted_iota(jnp.int32, (tokens_n, tokens_n), 0)
    c_io = lax.broadcasted_iota(jnp.int32, (tokens_n, tokens_n), 1)
    before = dot(hot_b, jnp.where(r_io < c_io, 1.0, 0.0).astype(BF16))
    before_b = before.astype(BF16)
    slots = N * CH
    s_r = lax.broadcasted_iota(jnp.int32, (slots, 32), 0)
    e_r = lax.broadcasted_iota(jnp.int32, (slots, 32), 1)
    to_slot = jnp.where(slot_expert(s_r, y, z, c) == e_r, 1.0, 0.0).astype(BF16)
    row_r = (lax.broadcasted_iota(jnp.int32, (slots, tokens_n), 0) & 15).astype(F32)
    here = (dot(to_slot, hot_b) > 0.5) & (dot(to_slot, before_b) == row_r)
    st[...] = jnp.where(here, 1.0, 0.0).astype(BF16)
    wt[...] = jnp.where(here, dot(to_slot, share), 0.0).astype(BF16)

    core_out, y_out, z_out, z_loc, far, near = {}, {}, {}, {}, {}, {}
    ag1, ag2, hid1, hid2 = {}, {}, {}, {}
    halves = (pl.ds(0, 1024), pl.ds(1024, dq - 1024))
    route = (pl.ds(0, dq // 2), pl.ds(dq // 2, dq // 2))
    rz_out, rz_loc, ry_out, rc_out, outs = {}, {}, {}, {}, []

    def remote(table, key, src, dst, send, recv, dev):
        cp = pltpu.make_async_remote_copy(
            src_ref=src, dst_ref=dst, send_sem=send, recv_sem=recv, device_id=dev, device_id_type=MESH
        )
        cp.start()
        table[key] = cp

    def dispatch(a, d):
        mat, rows = ((st, tok), (wt, cot))[a]
        made = dot(mat[d * CH : (d + 1) * CH, :], rows[...]).astype(BF16).reshape(2, 4, CAP, dq)
        xs[a, d, :, 0] = made[0]
        cs[a, d] = made[1]

    def send_core(a, d):
        remote(core_out, (a, d), cs.at[a, d], xs.at[a, d, :, 1], cos.at[a, d], cor.at[a, d], at(0, 0, 0, 1))

    def hop(axis, k):
        return at(0, k, 0, 0) if axis == 0 else at(0, 0, k, 0)

    def paths(d):
        for dy in (2, 1, 3, 0):
            off = (dy, (d - dy) % 4)
            for r in range(2):
                yield dy, r, off[r], off[1 - r]

    def send_y(a, d):
        core_out[a, d].wait_recv()
        for dy, r, f, g in paths(d):
            if f:
                w = route[r]
                remote(
                    y_out, (a, d, dy, r), xs.at[a, d, dy, :, :, w], (xr if g else xf).at[a, d, dy, :, :, w],
                    ys.at[a, d, dy, r], yr.at[a, d, dy, r], hop(r, f),
                )

    def send_z(a, d):
        if d == 0:
            z_loc[a] = pltpu.make_async_copy(xs.at[a, 0, 0], xf.at[a, 0, 0], loc.at[a])
            z_loc[a].start()
        for dy, r, f, g in sorted(paths(d), key=lambda p: p[2] % 4 == 2):
            if g:
                if f:
                    y_out[a, d, dy, r].wait_recv()
                w = route[r]
                remote(
                    z_out, (a, d, dy, r), (xr if f else xs).at[a, d, dy, :, :, w], xf.at[a, d, dy, :, :, w],
                    zs.at[a, d, dy, r], zr.at[a, d, dy, r], hop(1 - r, g),
                )

    def arrive(a, d):
        if d == 0:
            z_loc[a].wait()
        for dy, r, f, g in paths(d):
            if g:
                z_out[a, d, dy, r].wait_recv()
            elif f:
                y_out[a, d, dy, r].wait_recv()
        o = pltpu.make_async_copy(xf.at[a, d], (x_o, c_o)[a].at[d], xo_sem.at[a, d])
        o.start()
        outs.append(o)

    def scatter(t, d):
        buf, f_r, n_r = ((gu, gu_f, gu_n), (hh, hh_f, hh_n))[t]
        for i, dx in ((0, 1), (1, 3)):
            remote(far, (t, d, i), buf.at[d, xo, i], f_r.at[d, i], fs.at[t, d, i], fr.at[t, d, i], at(dx, 0, 0, 0))
        for i, (dx, q) in enumerate(((1, xp), (3, xm))):
            remote(
                near, (t, d, i), buf.at[d, q, 1 - i], n_r.at[d, i, 1 - i],
                ns.at[t, d, i], nr.at[t, d, i], at(dx, 0, 0, 0),
            )

    def scatter_on(t, d):
        buf, f_r, n_r = ((gu, gu_f, gu_n), (hh, hh_f, hh_n))[t]
        for i, (dx, q) in enumerate(((1, xp), (3, xm))):
            far[t, d, i].wait_recv()
            both = buf[d, q, i].astype(F32) + f_r[d, i].astype(F32)
            buf[d, q, i] = both.astype(BF16)
            remote(
                near, (t, d, 2 + i), buf.at[d, q, i], n_r.at[d, i, i],
                ns.at[t, d, 2 + i], nr.at[t, d, 2 + i], at(dx, 0, 0, 0),
            )

    def gate_up(d):
        arrive(0, d)
        if d == 0:
            weights[0].wait()
            weights[1].wait()
        rows = xf[0, d].reshape(CH, dq)
        gu[d, :, :, :, 0:ff] = dot(rows, wg[...]).astype(BF16).reshape(4, 2, CAP, ff)
        gu[d, :, :, :, ff : 2 * ff] = dot(rows, wu[...]).astype(BF16).reshape(4, 2, CAP, ff)
        scatter(0, d)

    def back(d):
        arrive(1, d)
        if d == 0:
            weights[2].wait()
        hh[d] = dot_nt(xf[1, d].reshape(CH, dq), wd[...]).astype(BF16).reshape(4, 2, CAP, ff)
        scatter(1, d)

    def finish(d):
        for t in range(2):
            for i in range(4):
                near[t, d, i].wait_recv()
        pre, gh = gu[d, x].astype(F32), hh[d, x].astype(F32)
        for i in range(2):
            pre = pre + gu_n[d, i].astype(F32)
            gh = gh + hh_n[d, i].astype(F32)
        g, u = pre[:, :, 0:ff], pre[:, :, ff : 2 * ff]
        sq = jax.nn.sigmoid(g)
        silu = g * sq
        hid[d, x] = (silu * u).astype(BF16)
        ag[d, x, :, :, 0:ff] = (gh * u * sq * (1.0 + g * (1.0 - sq))).astype(BF16)
        ag[d, x, :, :, ff : 2 * ff] = (gh * silu).astype(BF16)
        for i, dx in ((0, 1), (1, 3)):
            remote(ag1, (d, i), ag.at[d, x], ag.at[d, x], as1.at[d, i], ar1.at[d, i], at(dx, 0, 0, 0))

    def gather_on(d):
        for i, (dx, q) in enumerate(((1, xm), (3, xp))):
            ag1[d, i].wait_recv()
            remote(ag2, (d, i), ag.at[d, q, i], ag.at[d, q, i], as2.at[d, i], ar2.at[d, i], at(dx, 0, 0, 0))

    def hidden(d):
        for i, dx in ((0, 1), (1, 3)):
            remote(hid1, (d, i), hid.at[d, x], hid.at[d, x], hs1.at[d, i], hr1.at[d, i], at(dx, 0, 0, 0))

    def hidden_on(d):
        for i, (dx, q) in enumerate(((1, xm), (3, xp))):
            hid1[d, i].wait_recv()
            remote(hid2, (d, i), hid.at[d, q, i], hid.at[d, q, i], hs2.at[d, i], hr2.at[d, i], at(dx, 0, 0, 0))

    def keep(src, dst, sem):
        o = pltpu.make_async_copy(src, dst, sem)
        o.start()
        outs.append(o)

    def contrib(d, h):
        if h == 0:
            for i in range(2):
                ag2[d, i].wait_recv()
            for i, o_ref in enumerate((bg_o, bu_o)):
                keep(ag.at[d, :, :, :, pl.ds(i * ff, ff)], o_ref.at[d], ho_sem.at[i, d])
        w = halves[h]
        back_gate = ag[d, :, :, :, 0:ff].reshape(CH, ff)
        back_up = ag[d, :, :, :, ff : 2 * ff].reshape(CH, ff)
        total = dot_nt(back_gate, wg[w, :]) + dot_nt(back_up, wu[w, :])
        ct[d, :, :, :, w] = total.astype(BF16).reshape(4, 2, CAP, w.size)
        for dy, f, g in ways_back(d, h):
            if f:
                remote(
                    rz_out, (d, dy, h), ct.at[d, dy, :, :, w], (rz if g else rc).at[d, dy, :, :, w],
                    rzs.at[d, dy, h], rzr.at[d, dy, h], hop(1 - h, 4 - f),
                )
            elif g:
                second_back(ct, d, dy, h, g)
            else:
                rz_loc[h] = pltpu.make_async_copy(ct.at[d, 0, :, :, w], rc.at[d, 0, :, :, w], rloc.at[h])
                rz_loc[h].start()

    def ways_back(d, h):
        for dy in (2, 1, 3, 0):
            off = ((d - dy) % 4, dy)
            yield dy, off[h], off[1 - h]

    def second_back(src, d, dy, h, g):
        w = halves[h]
        remote(
            ry_out, (d, dy, h), src.at[d, dy, :, :, w], rc.at[d, dy, :, :, w],
            rys.at[d, dy, h], ryr.at[d, dy, h], hop(h, 4 - g),
        )

    def return_y(d, h):
        for dy, f, g in sorted(ways_back(d, h), key=lambda p: p[1] == 2):
            if f and g:
                rz_out[d, dy, h].wait_recv()
                second_back(rz, d, dy, h, g)

    def return_core(d, h):
        for dy, f, g in ways_back(d, h):
            if g:
                ry_out[d, dy, h].wait_recv()
            elif f:
                rz_out[d, dy, h].wait_recv()
            else:
                rz_loc[h].wait()
        w = halves[h]
        remote(
            rc_out, (d, h), rc.at[d, :, 1, :, w], rq.at[d, :, :, w], rcs.at[d, h], rcr.at[d, h], at(0, 0, 0, 1)
        )

    def combine(d):
        for h in range(2):
            rc_out[d, h].wait_recv()
        part = dot(sel[:, d * CH : d * CH + 64], rc[d, :, 0].reshape(64, dq))
        part = part + dot(sel[:, d * CH + 64 : (d + 1) * CH], rq[d].reshape(64, dq))
        if d == 0:
            acc[...] = part
        elif d < N - 1:
            acc[...] += part
        else:
            gt[...] = (acc[...] + part).astype(BF16)

    inputs[0].wait()
    dispatch(0, 0)
    pl.semaphore_wait(barrier, len(peers))
    send_core(0, 0)
    inputs[1].wait()
    dispatch(1, 0)
    send_core(1, 0)
    send_y(0, 0)
    dispatch(0, 1)
    send_core(0, 1)
    send_y(1, 0)
    dispatch(1, 1)
    send_core(1, 1)
    send_y(0, 1)
    send_z(0, 0)
    dispatch(0, 2)
    send_core(0, 2)
    send_y(1, 1)
    dispatch(1, 2)
    send_core(1, 2)
    dispatch(0, 3)
    send_core(0, 3)
    dispatch(1, 3)
    send_core(1, 3)
    sel[...] = st[...].astype(F32).T.astype(BF16)
    send_z(1, 0)
    send_y(0, 2)
    gate_up(0)
    send_z(0, 1)
    send_y(1, 2)
    back(0)
    scatter_on(0, 0)
    send_z(1, 1)
    send_y(0, 3)
    scatter_on(1, 0)
    gate_up(1)
    finish(0)
    send_z(0, 2)
    send_y(1, 3)
    back(1)
    scatter_on(0, 1)
    send_z(1, 2)
    gather_on(0)
    scatter_on(1, 1)
    gate_up(2)
    finish(1)
    send_z(0, 3)
    contrib(0, 0)
    back(2)
    contrib(0, 1)
    scatter_on(0, 2)
    send_z(1, 3)
    gather_on(1)
    scatter_on(1, 2)
    gate_up(3)
    return_y(0, 0)
    return_y(0, 1)
    back(3)
    finish(2)
    scatter_on(0, 3)
    contrib(1, 0)
    scatter_on(1, 3)
    gather_on(2)
    contrib(1, 1)
    finish(3)
    return_y(1, 0)
    contrib(2, 0)
    return_y(1, 1)
    gather_on(3)
    contrib(2, 1)
    return_y(2, 0)
    contrib(3, 0)
    hidden(0)
    hidden(1)
    return_y(2, 1)
    contrib(3, 1)
    hidden(2)
    hidden(3)
    return_core(0, 0)
    return_core(0, 1)
    return_core(1, 0)
    return_core(1, 1)
    combine(0)
    return_y(3, 0)
    return_y(3, 1)
    hidden_on(0)
    hidden_on(1)
    return_core(2, 0)
    return_core(2, 1)
    combine(1)
    hidden_on(2)
    hidden_on(3)
    return_core(3, 0)
    return_core(3, 1)
    combine(2)
    combine(3)
    for d in range(N):
        for i in range(2):
            hid2[d, i].wait_recv()
        keep(hid.at[d], hid_o.at[d], ho_sem.at[2, d])
    for table in (core_out, y_out, z_out, far, near, ag1, ag2, hid1, hid2, rz_out, ry_out, rc_out):
        for cp in table.values():
            cp.wait_send()
    for o in outs:
        o.wait()


def grads_body(x_ref, c_ref, hid, bg, bu, gg, gup, gd, hid_t):
    @pl.when(pl.program_id(0) == 0)
    def _():
        hid_t[...] = hid[...].T

    x_t = x_ref[...].T
    gg[...] = dot(x_t, bg[...]).astype(BF16)
    gup[...] = dot(x_t, bu[...]).astype(BF16)
    gd[...] = dot(hid_t[...], c_ref[...]).astype(BF16)


def grads(x_rows, c_rows, hid, bg, bu):
    slots, dq = x_rows.shape
    ff = hid.shape[1]
    tile = dq // 2
    sds = jax.ShapeDtypeStruct
    whole = pl.BlockSpec((slots, ff), lambda i: (0, 0))
    cols = pl.BlockSpec((slots, tile), lambda i: (0, i))
    rows = pl.BlockSpec((tile, ff), lambda i: (i, 0))
    return pl.pallas_call(
        grads_body,
        name="grads",
        grid=(dq // tile,),
        out_shape=(sds((dq, ff), BF16), sds((dq, ff), BF16), sds((ff, dq), BF16)),
        in_specs=[cols, cols, whole, whole, whole],
        out_specs=(rows, rows, pl.BlockSpec((ff, tile), lambda i: (0, i))),
        scratch_shapes=[pltpu.VMEM((ff, slots), BF16)],
        compiler_params=pltpu.CompilerParams(vmem_limit_bytes=60 * 2**20),
    )(x_rows, c_rows, hid, bg, bu)


def local(tokens, cotangent, expert_ids, gate_coef, w_gate, w_up, w_down):
    t_n, dq = tokens.shape
    ff = w_gate.shape[2]
    slots = N * CH
    vm = pl.BlockSpec(memory_space=pltpu.VMEM)
    anym = pl.BlockSpec(memory_space=pl.ANY)
    dma = pltpu.SemaphoreType.DMA
    sds = jax.ShapeDtypeStruct

    def rows(*shape):
        return pltpu.VMEM(shape, BF16)

    block = (4, 2, CAP)
    gt, x_o, c_o, hid, bg, bu = pl.pallas_call(
        body,
        name="exchange",
        out_shape=(
            sds((t_n, dq), BF16),
            sds((N, *block, dq), BF16),
            sds((N, *block, dq), BF16),
            sds((N, *block, ff), BF16),
            sds((N, *block, ff), BF16),
            sds((N, *block, ff), BF16),
        ),
        in_specs=[anym, anym, vm, vm, anym, anym, anym],
        out_specs=(vm, anym, anym, anym, anym, anym),
        scratch_shapes=[
            rows(t_n, dq),
            rows(t_n, dq),
            rows(dq, ff),
            rows(dq, ff),
            rows(ff, dq),
            rows(slots, t_n),
            rows(slots, t_n),
            rows(t_n, slots),
            pltpu.VMEM((t_n, dq), F32),
            rows(2, N, 4, CAP, dq),
            rows(2, N, *block, dq),
            rows(2, N, *block, dq),
            rows(2, N, *block, dq),
            rows(N, *block, 2 * ff),
            rows(N, *block, ff),
            rows(N, 2, CAP, 2 * ff),
            rows(N, 2, CAP, ff),
            rows(N, 2, 2, CAP, 2 * ff),
            rows(N, 2, 2, CAP, ff),
            rows(N, *block, 2 * ff),
            rows(N, *block, ff),
            rows(N, *block, dq),
            rows(N, *block, dq),
            rows(N, *block, dq),
            rows(N, 4, CAP, dq),
            dma((3,)),
            dma((2,)),
            dma((2, N)),
            dma((2, N)),
            dma((2, N, 4, 2)),
            dma((2, N, 4, 2)),
            dma((2, N, 4, 2)),
            dma((2, N, 4, 2)),
            dma((2,)),
            dma((2, N, 2)),
            dma((2, N, 2)),
            dma((2, N, 4)),
            dma((2, N, 4)),
            dma((N, 2)),
            dma((N, 2)),
            dma((N, 2)),
            dma((N, 2)),
            dma((N, 2)),
            dma((N, 2)),
            dma((N, 2)),
            dma((N, 2)),
            dma((N, 4, 2)),
            dma((N, 4, 2)),
            dma((2,)),
            dma((N, 4, 2)),
            dma((N, 4, 2)),
            dma((N, 2)),
            dma((N, 2)),
            dma((2, N)),
            dma((3, N)),
        ],
        compiler_params=pltpu.CompilerParams(
            collective_id=0, has_side_effects=True, vmem_limit_bytes=58 * 2**20
        ),
    )(tokens, cotangent, expert_ids.T, gate_coef.T, w_gate[0], w_up[0], w_down[0])
    grad_gate, grad_up, grad_down = grads(
        x_o.reshape(slots, dq),
        c_o.reshape(slots, dq),
        hid.reshape(slots, ff),
        bg.reshape(slots, ff),
        bu.reshape(slots, ff),
    )
    return (gt, grad_gate[None], grad_up[None], grad_down[None])


def solution(mesh):
    in_specs = (
        P("expert", "dp"),
        P("expert", "dp"),
        P("expert", None),
        P("expert", None),
        P("expert", "dp", None),
        P("expert", "dp", None),
        P("expert", None, "dp"),
    )
    out_specs = (
        P("expert", "dp"),
        P("expert", "dp", None),
        P("expert", "dp", None),
        P("expert", None, "dp"),
    )
    return jax.shard_map(local, mesh=mesh, in_specs=in_specs, out_specs=out_specs, check_vma=False)
```
